512 devices in a mesh: row: 8 (over y), col: 8 (over z_hi, x), depth: 8 (over z_lo, core).
Axes of the slice: x: 4, y: 8, z: 8 (z_hi: 2, z_lo: 4; z = z_hi * 4 + z_lo), core: 2. Of those that a mesh axis runs over, the one named last changes fastest.
Arguments:
- tokens: bfloat16 [512, 12288], P(('col', 'depth'), 'row'), may hold values from -6 to 6
- in_weight: bfloat16 [12288, 49152], P('row', ('col', 'depth')), may hold values from -0.0546875 to 0.0546875
- in_bias: bfloat16 [49152], P(('col', 'depth')), may hold values from -3 to 3
- out_weight: bfloat16 [49152, 12288], P(('col', 'depth'), 'row'), may hold values from -0.02734375 to 0.02734375
- out_bias: bfloat16 [12288], P('row'), may hold values from -3 to 3
Outputs:
- outputs: bfloat16 [512, 12288], P(('col', 'depth'), 'row')
The draws below stay inside these ranges and needn't reach their ends.
All inputs are finite; a program needn't handle non-finite values.
Results may differ from the reference program's by a relative error of at most 0.0044.
Values may be sent and summed in bfloat16 or wider, within the bound.
A program may use at most 64 MiB of HBM per device.

```python
import jax
import jax.numpy as jnp

D = 12288
FF = 49152
TOKENS = 512


def block_scale(key, dims, cuts, low, largest):
    level, own = 1.0, jax.random.fold_in(key, 6)
    for axis_at, parts in cuts:
        draws = jnp.exp(jax.random.uniform(jax.random.fold_in(own, axis_at), (parts,), jnp.float32, low / len(cuts), largest / len(cuts)))
        level = level * jnp.repeat(draws, dims[axis_at] // parts).reshape([-1 if axis == axis_at else 1 for axis in range(len(dims))])
    return level


def noise(rng, extent, deviation, bound, split=(), kind=jnp.bfloat16):
    array = jax.random.normal(rng, extent, jnp.float32) * deviation
    if len(split) > 0:
        array = block_scale(rng, extent, split, -0.22, 0.18) * array
    return jnp.clip(array, min=-bound, max=bound).astype(kind)


def setup_inputs(seed: int = 0) -> dict:
    key_of = jax.random.split(jax.random.key(seed), 6)
    return {
        "tokens": noise(key_of[0], (TOKENS, D), 1.0, 6.0, ((0, 64), (1, 8))),
        "in_weight": noise(key_of[1], (D, FF), D ** -0.5, 0.0546875, ((0, 8), (1, 64))),
        "in_bias": noise(key_of[2], (FF,), 0.5, 3.0, ((0, 64),)),
        "out_weight": noise(key_of[3], (FF, D), FF ** -0.5, 0.02734375, ((0, 64), (1, 8))),
        "out_bias": noise(key_of[4], (D,), 0.5, 3.0, ((0, 8),)),
    }


def reference(tokens, in_weight, in_bias, out_weight, out_bias):
    pre = jnp.dot(tokens, in_weight, preferred_element_type=jnp.float32) + in_bias.astype(jnp.float32)
    hidden = jax.nn.gelu(pre, approximate=True).astype(jnp.bfloat16)
    summed = jnp.dot(hidden, out_weight, preferred_element_type=jnp.float32) + out_bias.astype(jnp.float32)
    return summed.astype(jnp.bfloat16)
```

```python
import jax
import jax.numpy as jnp
from jax import lax
from jax.experimental import pallas as pl
from jax.experimental.pallas import tpu as pltpu
from jax.sharding import PartitionSpec as P

BF, F32 = jnp.bfloat16, jnp.float32
H = 768
NB = 3
W = H // NB


def kernel(tok_ref, w1_ref, b1_ref, w2_ref, b2_ref, out_ref,
           w1v, w2v, tsend, trecv, tok, pm, s_a, s_b, r_a, r_b, hid, po, os_, xr, zs, zr, zown, fs, fr,
           lsem, wsem, tsem, zsem, zsend, xsem, xsend, csem, csend,
           ra_sem, rb_sem, rsend, ha_sem, hb_sem, hsend, hc_sem, hcsend,
           ox_sem, oxsend, oz_sem, ozsend, fsem):
    y = lax.axis_index("row")
    col = lax.axis_index("col")
    dep = lax.axis_index("depth")
    x = col % 4
    z = (col // 4) * 4 + dep // 2
    c = dep % 2
    sg = 1 - 2 * c

    def dev(dx=0, dy=0, dz=0, dc=0):
        px, py, pz, pc = (x + dx) % 4, (y + dy + 8) % 8, (z + dz) % 8, (c + dc) % 2
        return {"row": py, "col": (pz // 4) * 4 + px, "depth": (pz % 4) * 2 + pc}

    def send(src, dst, ssem, rsem, to):
        pltpu.make_async_remote_copy(
            src_ref=src, dst_ref=dst, send_sem=ssem, recv_sem=rsem,
            device_id=to, device_id_type=pl.DeviceIdType.MESH).start()

    def wait(ref, sem):
        pltpu.make_async_copy(ref, ref, sem).wait()

    other = dev(dc=1)
    w1_copy = pltpu.make_async_copy(w1_ref, w1v, lsem.at[0])
    w1_copy.start()
    w2_copy = pltpu.make_async_copy(
        w2_ref.at[:, pl.ds(pl.multiple_of(c * H, H), H)], w2v.at[c], lsem.at[1])
    w2_copy.start()

    barrier = pltpu.get_barrier_semaphore()
    partners = [other, dev(dy=1), dev(dy=-1)]
    partners += [dev(dx=e) for e in (1, 2, 3)] + [dev(dz=d) for d in range(1, 8)]
    for to in partners:
        pl.semaphore_signal(barrier, inc=1, device_id=to, device_id_type=pl.DeviceIdType.MESH)
    pl.semaphore_wait(barrier, len(partners))

    left = tok_ref[:, :H].astype(F32)
    right = tok_ref[:, H:].astype(F32)
    first = c == 0
    tsend[...] = jnp.where(first, right, left)
    send(tsend, trecv, tsem.at[0], tsem.at[1], other)
    send(w2_ref.at[:, pl.ds(pl.multiple_of((1 - c) * H, H), H)], w2v.at[c], wsem.at[0], wsem.at[1], other)
    mine = jnp.where(first, left, right)

    def slot_of(pz, s):
        g = (s * (pz - y) + 23) % 8
        hi = g // 4
        return (1 - hi) * (6 - 2 * g) + hi * (2 * g - 7)

    def rows_of(pz, s, n, off=0):
        return pl.ds(pl.multiple_of(slot_of(pz, s) * 64 + off, 16), n)

    wait(trecv, tsem.at[1])
    theirs = trecv[...]
    own_rows = tok.at[c, rows_of(z, sg, 16, x * 16)]
    own_rows[...] = jnp.concatenate(
        [jnp.where(first, mine, theirs), jnp.where(first, theirs, mine)], axis=0).astype(BF)

    order = (4, 3, 5, 2, 6, 1, 7)
    for d in order:
        send(own_rows, own_rows, zsend, zsem.at[d], dev(dz=d))
    for d in (0, 1, 7, 2, 6, 3, 5, 4):
        piece = tok.at[c, rows_of(z - d + 8, sg, 16, x * 16)]
        if d:
            wait(piece, zsem.at[d])
        for e in (2, 1, 3):
            send(piece, piece, xsend, xsem.at[d, e - 1], dev(dx=e))
    for d in (0, 1, 7, 2, 6, 3, 5, 4):
        for e in (1, 3, 2):
            wait(tok.at[c, rows_of(z - d + 8, sg, 16, ((x - e + 4) % 4) * 16)], xsem.at[d, e - 1])
        send(tok.at[c, rows_of(z - d + 8, sg, 64)], tok.at[c, rows_of(z - d + 8, -sg, 64)],
             csend, csem.at[d], other)
    w1_copy.wait()
    for d in range(8):
        wait(tok.at[1 - c, rows_of(z - d + 8, sg, 64)], csem.at[d])

    def product(s, cols):
        rows = slice(s * 128, s * 128 + 128)
        return (jnp.dot(tok[0, rows, :], w1v[:H, cols], preferred_element_type=F32)
                + jnp.dot(tok[1, rows, :], w1v[H:, cols], preferred_element_type=F32))

    ahead, back = dev(dy=sg), dev(dy=-sg)
    for s in range(4):
        if s:
            for n in range(NB):
                cols = slice(n * W, n * W + W)
                pm[s * 128:s * 128 + 128, cols] = product(s, cols)
        for n in range(NB):
            cols = slice(n * W, n * W + W)
            if s == 0:
                part = product(0, cols)
                part_a, part_b = part[:64], part[64:]
            else:
                wait(r_a.at[s - 1, :, cols], ra_sem.at[s - 1, n])
                part_a = pm[s * 128:s * 128 + 64, cols] + r_a[s - 1, :, cols].astype(F32)
            s_a[s, :, cols] = part_a.astype(BF)
            send(s_a.at[s, :, cols], r_a.at[s, :, cols], rsend.at[0], ra_sem.at[s, n], ahead)
            if s:
                wait(r_b.at[s - 1, :, cols], rb_sem.at[s - 1, n])
                part_b = pm[s * 128 + 64:s * 128 + 128, cols] + r_b[s - 1, :, cols].astype(F32)
            if s < 3:
                s_b[s, :, cols] = part_b.astype(BF)
                send(s_b.at[s, :, cols], r_b.at[s, :, cols], rsend.at[1], rb_sem.at[s, n], back)
            else:
                pm[448:512, cols] = part_b

    def chunk(slot, cols):
        return hid.at[c, pl.ds(pl.multiple_of(slot * 64, 64), 64), cols]

    for n in range(NB):
        cols = slice(n * W, n * W + W)
        wait(r_a.at[3, :, cols], ra_sem.at[3, n])
        v = pm[448:512, cols] + r_a[3, :, cols].astype(F32) + b1_ref[:, cols].astype(F32)
        chunk(0, cols)[...] = jax.nn.gelu(v, approximate=True).astype(BF)
        send(chunk(0, cols), chunk(2 - c, cols), hsend.at[0], ha_sem.at[0, n], ahead)
        send(chunk(0, cols), chunk(1 + c, cols), hsend.at[1], hb_sem.at[0, n], back)
        send(chunk(0, cols), chunk(0, cols), hcsend, hc_sem.at[0, n], other)

    w2_copy.wait()
    wait(w2v.at[1 - c], wsem.at[1])

    def second(slot, count):
        rows = slice(slot * 64, (slot + count) * 64)
        po[rows, :] = (jnp.dot(hid[0, rows, :], w2v[0], preferred_element_type=F32)
                       + jnp.dot(hid[1, rows, :], w2v[1], preferred_element_type=F32))
        os_[rows, :] = po[rows, :].astype(BF)
        for k in range(slot, slot + count):
            for e in (2, 1, 3):
                part = pl.ds(pl.multiple_of(k * 64 + ((x + e) % 4) * 16, 16), 16)
                send(os_.at[part], xr.at[k, e - 1], oxsend, ox_sem.at[k, e - 1], dev(dx=e))

    def arrived(slot):
        for n in range(NB):
            cols = slice(n * W, n * W + W)
            wait(hid.at[1 - c, slot * 64:slot * 64 + 64, cols], hc_sem.at[slot, n])

    rel = (0, 1, -1, 2, -2, 3, -3, 4)

    def along_z(k):
        mine = po[pl.ds(pl.multiple_of(k * 64 + x * 16, 16), 16), :]
        for e in (1, 3, 2):
            wait(xr.at[k, e - 1], ox_sem.at[k, e - 1])
            mine = mine + xr[k, e - 1].astype(F32)
        zs[k] = mine.astype(BF)
        d = (y + rel[k] - z + 16) % 8

        @pl.when(d == 0)
        def _():
            zown[...] = mine

        @pl.when(d != 0)
        def _():
            send(zs.at[k], zr.at[d], ozsend, oz_sem.at[d], dev(dz=d))

    pairs = ((0, 1), (1, 2), (3, 2), (5, 2), (7, 1))
    for j in range(1, 5):
        for n in range(NB):
            cols = slice(n * W, n * W + W)
            at = 7 if j == 4 else 2 * j - c
            wait(chunk(at, cols), ha_sem.at[j - 1, n])
            if j < 4:
                to = 7 if j == 3 else 2 * j + 2 - c
                send(chunk(at, cols), chunk(to, cols), hsend.at[0], ha_sem.at[j, n], ahead)
            send(chunk(at, cols), chunk(at, cols), hcsend, hc_sem.at[at, n], other)
            if j < 4:
                at = 2 * j - 1 + c
                wait(chunk(at, cols), hb_sem.at[j - 1, n])
                if j < 3:
                    send(chunk(at, cols), chunk(2 * j + 1 + c, cols), hsend.at[1], hb_sem.at[j, n], back)
                send(chunk(at, cols), chunk(at, cols), hcsend, hc_sem.at[at, n], other)
        slot, count = pairs[j - 1]
        for k in range(slot, slot + count):
            arrived(k)
        second(slot, count)
        if j > 1:
            slot, count = pairs[j - 2]
            for k in range(slot, slot + count):
                along_z(k)
    arrived(7)
    second(7, 1)
    for k in (5, 6, 7):
        along_z(k)

    total = zown[...]
    for d in (1, 7, 2, 6, 3, 5, 4):
        wait(zr.at[d], oz_sem.at[d])
        total = total + zr[d].astype(F32)
    fs[...] = jnp.where(first, total[8:], total[:8])
    send(fs, fr, fsem.at[0], fsem.at[1], other)
    mine = jnp.where(first, total[:8], total[8:])
    wait(fr, fsem.at[1])
    theirs = fr[...]
    out_ref[:, :H] = (jnp.where(first, mine, theirs) + b2_ref[:, :H].astype(F32)).astype(BF)
    out_ref[:, H:] = (jnp.where(first, theirs, mine) + b2_ref[:, H:].astype(F32)).astype(BF)

    wait(tsend, tsem.at[0])
    wait(w2v.at[0], wsem.at[0])
    wait(tok.at[0, :112], zsend)
    wait(tok.at[0, :384], xsend)
    wait(tok.at[0], csend)
    wait(tok.at[0, :256], rsend.at[0])
    wait(tok.at[0, :192], rsend.at[1])
    wait(tok.at[0, :256], hsend.at[0])
    wait(tok.at[0, :192], hsend.at[1])
    wait(tok.at[0], hcsend)
    wait(tok.at[0, :384], oxsend)
    wait(tok.at[0, :112], ozsend)
    wait(fs, fsem.at[0])


def local(tokens, in_weight, in_bias, out_weight, out_bias):
    vm = pl.BlockSpec(memory_space=pltpu.VMEM)
    hbm = pl.BlockSpec(memory_space=pl.ANY)
    dma = pltpu.SemaphoreType.DMA
    return pl.pallas_call(
        kernel,
        out_shape=jax.ShapeDtypeStruct((8, 2 * H), BF),
        in_specs=[vm, hbm, vm, hbm, vm],
        out_specs=vm,
        scratch_shapes=[
            pltpu.VMEM((2 * H, H), BF), pltpu.VMEM((2, H, H), BF),
            pltpu.VMEM((8, H), F32), pltpu.VMEM((8, H), F32),
            pltpu.VMEM((2, 512, H), BF), pltpu.VMEM((512, H), F32),
            pltpu.VMEM((4, 64, H), BF), pltpu.VMEM((3, 64, H), BF),
            pltpu.VMEM((4, 64, H), BF), pltpu.VMEM((3, 64, H), BF),
            pltpu.VMEM((2, 512, H), BF),
            pltpu.VMEM((512, H), F32), pltpu.VMEM((512, H), BF),
            pltpu.VMEM((8, 3, 16, H), BF), pltpu.VMEM((8, 16, H), BF),
            pltpu.VMEM((8, 16, H), BF), pltpu.VMEM((16, H), F32),
            pltpu.VMEM((8, H), F32), pltpu.VMEM((8, H), F32),
            dma((2,)), dma((2,)), dma((2,)), dma((8,)), dma, dma((8, 3)), dma, dma((8,)), dma,
            dma((4, NB)), dma((3, NB)), dma((2,)), dma((4, NB)), dma((3, NB)), dma((2,)),
            dma((8, NB)), dma, dma((8, 3)), dma, dma((8,)), dma, dma((2,)),
        ],
        compiler_params=pltpu.CompilerParams(
            collective_id=0, has_side_effects=True, vmem_limit_bytes=60 * 2**20),
    )(tokens, in_weight, in_bias.reshape(1, H), out_weight, out_bias.reshape(1, 2 * H))


def solution(mesh):
    in_specs = (
        P(("col", "depth"), "row"),
        P("row", ("col", "depth")),
        P(("col", "depth")),
        P(("col", "depth"), "row"),
        P("row"),
    )
    out_specs = P(("col", "depth"), "row")
    return jax.shard_map(local, mesh=mesh, in_specs=in_specs, out_specs=out_specs, check_vma=False)
```
